32 devices in a mesh: blk: 8 (over z, core), layer: 4 (over y, x).
Axes of the slice: x: 2, y: 2, z: 4, core: 2. Of those that a mesh axis runs over, the one named last changes fastest.
Arguments:
- t2: bfloat16 [1024, 8, 4, 1024], P(None, 'blk', 'layer'), may hold values from -6 to 6
- tile_ids: int32 [8, 4, 8], P('blk', 'layer'), may hold values from 0 to 7, each once within a row
- counts: int32 [8, 4], P('blk', 'layer'), may hold values from 4 to 8, as said below
- integrals: bfloat16 [8, 4, 4, 8, 128, 1024], P('blk', 'layer'), may hold values from -0.09375 to 0.09375
- owner: int32 [8, 4], P('blk'), may hold values from 0 to 3, each once within a row
Outputs:
- residual: bfloat16 [4, 256, 8, 1024], P('layer', None, 'blk')
The draws below stay inside these ranges and needn't reach their ends.
Inputs may be any that keep to these rules, and one draw needn't show every extreme that they name: Slots j >= counts hold no tile and are ignored; some group is full in every draw.
All inputs are finite; a program needn't handle non-finite values.
Results may differ from the reference program's by a relative error of at most 0.001.
Values may be sent and summed in bfloat16 or wider, within the bound.
A program may use at most 128 MiB of HBM per device.

```python
import jax
import jax.numpy as jnp
from jax import lax

TILE = 128
KT_DEV = 8
STOPS = 4
P_DEV = 256
ROWS = 1024
COLS = 1024
N_BLK = 8
N_LAYER = 4


def draw_counts(key, part):
    first = jax.random.fold_in(key, 11)
    second = jax.random.fold_in(key, 23)
    values = jax.random.randint(first, (N_BLK, N_LAYER), KT_DEV // 2, KT_DEV + 1).astype(jnp.int32)
    chosen = jax.random.randint(second, (), 0, N_BLK * N_LAYER).astype(jnp.int32)
    flat_index = jnp.arange(N_BLK * N_LAYER, dtype=jnp.int32).reshape(N_BLK, N_LAYER)
    return jnp.where(flat_index == chosen, KT_DEV, values).astype(jnp.int32)


def level_of(rng, dims, cuts, least, top_value):
    level, own = 1.0, jax.random.fold_in(rng, 6)
    for axis_at, parts in cuts:
        heights = jnp.exp(jax.random.uniform(jax.random.fold_in(own, axis_at), (parts,), jnp.float32, least / len(cuts), top_value / len(cuts)))
        level = level * jnp.repeat(heights, dims[axis_at] // parts).reshape([-1 if axis == axis_at else 1 for axis in range(len(dims))])
    return level


def noise(key, dims, spread, most, pieces=(), held_as=jnp.bfloat16):
    values = spread * jax.random.normal(key, dims, jnp.float32)
    if pieces:
        values = values * level_of(key, dims, pieces, -0.22, 0.18)
    return jnp.clip(values, -most, most).astype(held_as)


def setup_inputs(seed: int = 0) -> dict:
    key_of = jax.random.split(jax.random.key(seed), 6)
    t2 = noise(key_of[0], (ROWS, N_BLK, N_LAYER, KT_DEV * TILE), 1.0, 6.0, ((1, 8), (2, 4)))
    tile_ids = jax.vmap(lambda own: jax.random.permutation(own, KT_DEV))(jax.random.split(key_of[1], N_BLK * N_LAYER)).reshape((N_BLK, N_LAYER, KT_DEV)).astype(jnp.int32)
    counts = draw_counts(jax.random.fold_in(key_of[5], 71), 0)
    integrals = noise(key_of[3], (N_BLK, N_LAYER, STOPS, KT_DEV, TILE, COLS), (STOPS * KT_DEV * TILE) ** -0.5, 0.09375, ((0, 8), (1, 4)))
    owner = jax.vmap(lambda own: jax.random.permutation(own, N_LAYER))(jax.random.split(key_of[4], N_BLK)).reshape((N_BLK, N_LAYER)).astype(jnp.int32)
    return {"t2": t2, "tile_ids": tile_ids, "counts": counts, "integrals": integrals, "owner": owner}


def expand_group(t2, tile_ids, counts, grp_index, lay_index):
    slot_index = jnp.arange(KT_DEV, dtype=jnp.int32)
    column = lax.dynamic_index_in_dim(t2, grp_index, 1, keepdims=False)
    column = lax.dynamic_index_in_dim(column, lay_index, 1, keepdims=False)
    column = column.astype(jnp.float32).reshape(ROWS, KT_DEV, TILE)
    ids_row = tile_ids[grp_index, lay_index]
    filled = counts[grp_index, lay_index]
    select = (ids_row[:, None] == slot_index[None, :]) & (slot_index < filled)[:, None]
    placed = jnp.einsum("pjt,jk->pkt", column, select.astype(jnp.float32), precision=lax.Precision.HIGHEST)
    return placed.reshape(ROWS, KT_DEV * TILE)


def reference(t2, tile_ids, counts, integrals, owner):
    def per_block(blk_index):
        summed = jnp.zeros((ROWS, COLS), jnp.float32)
        slab = lax.dynamic_index_in_dim(integrals, blk_index, 0, keepdims=False)
        for lay_index in range(N_LAYER):
            for stop_index in range(STOPS):
                source = ((blk_index - stop_index) % N_BLK).astype(jnp.int32)
                placed = expand_group(t2, tile_ids, counts, source, lay_index)
                block = slab[lay_index, stop_index].astype(jnp.float32).reshape(KT_DEV * TILE, COLS)
                summed = summed + jnp.dot(placed, block, preferred_element_type=jnp.float32, precision=lax.Precision.HIGHEST)
        return summed

    partial_value = lax.map(per_block, jnp.arange(N_BLK, dtype=jnp.int32))
    partial_value = partial_value.reshape(N_BLK, N_LAYER, P_DEV, COLS)
    inverse = jnp.argsort(owner, axis=1).astype(jnp.int32)
    partial_value = jnp.take_along_axis(partial_value, inverse[:, :, None, None], axis=1)
    return jnp.transpose(partial_value, (1, 2, 0, 3)).astype(jnp.bfloat16)
```

```python
import functools

import jax
import jax.numpy as jnp
from jax import lax
from jax.experimental import pallas as pl
from jax.experimental.pallas import tpu as pltpu
from jax.sharding import PartitionSpec as P

MESH = pl.DeviceIdType.MESH
LANES = 256
CHUNK_ROWS = 32
ACC_SLOTS = 4


def kernel(
    n_blk,
    n_layer,
    ids_ref,
    counts_ref,
    owner_ref,
    t2_ref,
    ints_ref,
    out_ref,
    packed,
    panels,
    slab,
    acc,
    stage,
    landed,
    t2_sem,
    slab_sem,
    ring_send,
    ring_recv,
    sum_send,
    sum_recv,
):
    stops = ints_ref.shape[0]
    tile_rows, width = t2_ref.shape[1], t2_ref.shape[2]
    cols = ints_ref.shape[2]
    tiles = ids_ref.shape[0]
    tile = width // tiles
    rows = panels.shape[3]
    chunks = tile_rows // rows
    lanes = min(LANES, cols)
    blk, layer = lax.axis_index("blk"), lax.axis_index("layer")
    right, left = lax.rem(blk + 1, n_blk), lax.rem(blk + n_blk - 1, n_blk)
    others = [lax.rem(layer + d, n_layer) for d in range(1, n_layer)]

    t2_copy = pltpu.make_async_copy(t2_ref, packed, t2_sem)
    t2_copy.start()
    slab_copies = [
        pltpu.make_async_copy(ints_ref.at[s], slab.at[s], slab_sem.at[s]) for s in range(stops)
    ]
    for copy in slab_copies:
        copy.start()

    barrier = pltpu.get_barrier_semaphore()
    for neighbour in (left, right):
        pl.semaphore_signal(barrier, inc=1, device_id={"blk": neighbour}, device_id_type=MESH)
    for other in others:
        pl.semaphore_signal(barrier, inc=1, device_id={"layer": other}, device_id_type=MESH)

    count = counts_ref[0]

    def weight(condition, dtype):
        return jnp.full((1, tile), condition.astype(jnp.float32), jnp.float32).astype(dtype)

    def expand(c):
        pieces = [
            packed[:, pl.ds(c * rows, rows), j * tile : (j + 1) * tile].reshape(n_layer * rows, tile)
            for j in range(tiles)
        ]
        for k in range(tiles):
            placed = pieces[0] * held[0][k]
            for j in range(1, tiles):
                placed = placed + pieces[j] * held[j][k]
            panels[0, c, :, :, k * tile : (k + 1) * tile] = placed.reshape(n_layer, rows, tile)

    def to_slots(c):
        for q in range(n_layer):
            for n in range(cols // tile):
                at = slice(n * tile, (n + 1) * tile)
                moved = acc[c % ACC_SLOTS, 0, :, at] * owned[0][q]
                for t in range(1, n_layer):
                    moved = moved + acc[c % ACC_SLOTS, t, :, at] * owned[t][q]
                stage[c, q, :, at] = moved

    def hop(s, c):
        return pltpu.make_async_remote_copy(
            src_ref=panels.at[s, c],
            dst_ref=panels.at[s + 1, c],
            send_sem=ring_send.at[s, c],
            recv_sem=ring_recv.at[s, c],
            device_id={"blk": right},
            device_id_type=MESH,
        )

    def give(d, c):
        return pltpu.make_async_remote_copy(
            src_ref=stage.at[c, others[d]],
            dst_ref=landed.at[d, c],
            send_sem=sum_send.at[d, c],
            recv_sem=sum_recv.at[d, c],
            device_id={"layer": others[d]},
            device_id_type=MESH,
        )

    def multiply(s, c, first):
        @pl.loop(0, cols // lanes)
        def _(n):
            at = pl.ds(pl.multiple_of(n * lanes, lanes), lanes)
            left_side = panels[s, c].reshape(n_layer * rows, width)
            product = jnp.dot(left_side, slab[s, :, at], preferred_element_type=jnp.float32)
            product = product.reshape(n_layer, rows, lanes)
            if first:
                acc[c % ACC_SLOTS, :, :, at] = product
            else:
                acc[c % ACC_SLOTS, :, :, at] += product

    def finish(c):
        for d in range(n_layer - 1):
            give(d, c).wait_recv()
        total = stage[c, layer]
        for d in range(n_layer - 1):
            total = total + landed[d, c]
        out_ref[c * rows : (c + 1) * rows, :] = total.astype(out_ref.dtype)

    held = [
        [weight((ids_ref[j] == k) & (j < count), jnp.bfloat16) for k in range(tiles)]
        for j in range(tiles)
    ]
    owned = [
        [weight(owner_ref[t] == q, jnp.float32) for q in range(n_layer)] for t in range(n_layer)
    ]
    t2_copy.wait()
    for c in range(min(2, chunks)):
        expand(c)
    pl.semaphore_wait(barrier, 2 + n_layer - 1)
    for c in range(min(2, chunks)):
        hop(0, c).start()
    for c in range(2, chunks):
        expand(c)

    hops = stops - 1
    for step in range(chunks + hops - 1):
        for s in range(1, hops):
            c = step - (s - 1)
            if 0 <= c < chunks:
                hop(s - 1, c).wait_recv()
                hop(s, c).start()
        if step + 2 < chunks:
            hop(0, step + 2).start()
        if step == 0:
            slab_copies[0].wait()
        if step < chunks:
            multiply(0, step, True)
        for s in range(1, hops):
            c = step - (s - 1)
            if c == 0:
                slab_copies[s].wait()
            if 0 <= c < chunks:
                multiply(s, c, False)
        c = step - (hops - 1)
        if c == 0:
            slab_copies[hops].wait()
        if 0 <= c < chunks:
            hop(hops - 1, c).wait_recv()
            multiply(hops, c, False)
            to_slots(c)
            for d in range(n_layer - 1):
                give(d, c).start()
        if 0 <= c - 2 < chunks:
            finish(c - 2)
    for c in range(max(chunks - 2, 0), chunks):
        finish(c)
    for c in range(chunks):
        for s in range(hops):
            hop(s, c).wait_send()
        for d in range(n_layer - 1):
            give(d, c).wait_send()


def body(n_blk, n_layer, t2, tile_ids, counts, integrals, owner):
    row_count, width = t2.shape[0], t2.shape[3]
    stops, tiles, tile, cols = integrals.shape[2:]
    tile_rows = row_count // n_layer
    rows = CHUNK_ROWS
    chunks = tile_rows // rows
    hops = stops - 1
    moved = 2 * stops * width * cols + 2 * row_count * width
    result = pl.pallas_call(
        functools.partial(kernel, n_blk, n_layer),
        out_shape=jax.ShapeDtypeStruct((tile_rows, cols), jnp.bfloat16),
        in_specs=[pl.BlockSpec(memory_space=pltpu.SMEM)] * 3 + [pl.BlockSpec(memory_space=pl.ANY)] * 2,
        out_specs=pl.BlockSpec(memory_space=pltpu.VMEM),
        scratch_shapes=[
            pltpu.VMEM((n_layer, tile_rows, width), jnp.bfloat16),
            pltpu.VMEM((stops, chunks, n_layer, rows, width), jnp.bfloat16),
            pltpu.VMEM((stops, width, cols), jnp.bfloat16),
            pltpu.VMEM((ACC_SLOTS, n_layer, rows, cols), jnp.float32),
            pltpu.VMEM((chunks, n_layer, rows, cols), jnp.float32),
            pltpu.VMEM((n_layer - 1, chunks, rows, cols), jnp.float32),
            pltpu.SemaphoreType.DMA,
            pltpu.SemaphoreType.DMA((stops,)),
            pltpu.SemaphoreType.DMA((hops, chunks)),
            pltpu.SemaphoreType.DMA((hops, chunks)),
            pltpu.SemaphoreType.DMA((n_layer - 1, chunks)),
            pltpu.SemaphoreType.DMA((n_layer - 1, chunks)),
        ],
        compiler_params=pltpu.CompilerParams(
            collective_id=0, has_side_effects=True, vmem_limit_bytes=60 * 2**20
        ),
        cost_estimate=pl.CostEstimate(
            flops=2 * stops * row_count * width * cols, bytes_accessed=moved, transcendentals=0
        ),
    )(
        tile_ids.reshape(tiles),
        counts.reshape(1),
        owner.reshape(n_layer),
        t2.reshape(n_layer, tile_rows, width),
        integrals.reshape(stops, tiles * tile, cols),
    )
    return result.reshape(1, tile_rows, 1, cols)


def solution(mesh):
    return jax.shard_map(
        functools.partial(body, mesh.shape["blk"], mesh.shape["layer"]),
        mesh=mesh,
        in_specs=(
            P(None, "blk", "layer", None),
            P("blk", "layer", None),
            P("blk", "layer"),
            P("blk", "layer", None, None, None, None),
            P("blk", None),
        ),
        out_specs=P("layer", None, "blk", None),
        check_vma=False,
    )
```

```python
import functools

import jax
import jax.numpy as jnp
from jax import lax
from jax.experimental import pallas as pl
from jax.experimental.pallas import tpu as pltpu
from jax.sharding import PartitionSpec as P

MESH = pl.DeviceIdType.MESH
LANES = 256
ACC_SLOTS = 4
AHEAD = 2
SIXTEENTHS = (1, 2, 2, 2, 2, 2, 2, 1, 1, 1)


def kernel(
    n_blk,
    n_layer,
    ids_ref,
    counts_ref,
    owner_ref,
    t2_ref,
    ints_ref,
    out_ref,
    head,
    rest,
    panels,
    slab,
    acc,
    stage,
    landed,
    t2_sem,
    slab_sem,
    ring_send,
    ring_recv,
    sum_send,
    sum_recv,
):
    stops = ints_ref.shape[0]
    tile_rows, width = t2_ref.shape[1], t2_ref.shape[2]
    cols = ints_ref.shape[2]
    tiles = ids_ref.shape[0]
    tile = width // tiles
    sizes = [part * tile_rows // 16 for part in SIXTEENTHS]
    starts = [sum(sizes[:c]) for c in range(len(sizes))]
    chunks = len(sizes)
    lanes = min(LANES, cols)
    blk, layer = lax.axis_index("blk"), lax.axis_index("layer")
    right, left = lax.rem(blk + 1, n_blk), lax.rem(blk + n_blk - 1, n_blk)
    others = [lax.rem(layer + d, n_layer) for d in range(1, n_layer)]

    barrier = pltpu.get_barrier_semaphore()
    for neighbour in (left, right):
        pl.semaphore_signal(barrier, inc=1, device_id={"blk": neighbour}, device_id_type=MESH)
    for other in others:
        pl.semaphore_signal(barrier, inc=1, device_id={"layer": other}, device_id_type=MESH)

    t2_copies = [
        pltpu.make_async_copy(t2_ref.at[:, pl.ds(0, sizes[0])], head, t2_sem.at[0]),
        pltpu.make_async_copy(
            t2_ref.at[:, pl.ds(sizes[0], tile_rows - sizes[0])], rest, t2_sem.at[1]
        ),
    ]
    slab_copies = [
        pltpu.make_async_copy(ints_ref.at[s], slab.at[s], slab_sem.at[s]) for s in range(stops)
    ]
    for copy in t2_copies + slab_copies:
        copy.start()

    count = counts_ref[0]

    def weight(condition, dtype):
        return jnp.full((1, tile), condition.astype(jnp.float32), jnp.float32).astype(dtype)

    def span(c):
        return pl.ds(n_layer * starts[c], n_layer * sizes[c])

    def expand(c):
        source, at = (head, 0) if c == 0 else (rest, starts[c] - sizes[0])
        pieces = [
            source[:, pl.ds(at, sizes[c]), j * tile : (j + 1) * tile].reshape(n_layer * sizes[c], tile)
            for j in range(tiles)
        ]
        for k in range(tiles):
            placed = pieces[0] * held[0][k]
            for j in range(1, tiles):
                placed = placed + pieces[j] * held[j][k]
            panels[0, span(c), k * tile : (k + 1) * tile] = placed

    def to_slots(c):
        for q in range(n_layer):
            for n in range(cols // tile):
                at = slice(n * tile, (n + 1) * tile)
                moved = acc[c % ACC_SLOTS, pl.ds(0, sizes[c]), at] * owned[0][q]
                for t in range(1, n_layer):
                    moved = moved + acc[c % ACC_SLOTS, pl.ds(t * sizes[c], sizes[c]), at] * owned[t][q]
                stage[q, pl.ds(starts[c], sizes[c]), at] = moved

    def hop(s, c):
        return pltpu.make_async_remote_copy(
            src_ref=panels.at[s, span(c)],
            dst_ref=panels.at[s + 1, span(c)],
            send_sem=ring_send.at[s, c],
            recv_sem=ring_recv.at[s, c],
            device_id={"blk": right},
            device_id_type=MESH,
        )

    def give(d, c):
        return pltpu.make_async_remote_copy(
            src_ref=stage.at[others[d], pl.ds(starts[c], sizes[c])],
            dst_ref=landed.at[d, pl.ds(starts[c], sizes[c])],
            send_sem=sum_send.at[d, c],
            recv_sem=sum_recv.at[d, c],
            device_id={"layer": others[d]},
            device_id_type=MESH,
        )

    def multiply(s, c, first):
        @pl.loop(0, cols // lanes)
        def _(n):
            at = pl.ds(pl.multiple_of(n * lanes, lanes), lanes)
            product = jnp.dot(
                panels[s, span(c)], slab[s, :, at], preferred_element_type=jnp.float32
            )
            if first:
                acc[c % ACC_SLOTS, pl.ds(0, n_layer * sizes[c]), at] = product
            else:
                acc[c % ACC_SLOTS, pl.ds(0, n_layer * sizes[c]), at] += product

    def finish(c):
        for d in range(n_layer - 1):
            give(d, c).wait_recv()
        at = pl.ds(starts[c], sizes[c])
        total = stage[layer, at]
        for d in range(n_layer - 1):
            total = total + landed[d, at]
        out_ref[at, :] = total.astype(out_ref.dtype)

    held = [
        [weight((ids_ref[j] == k) & (j < count), jnp.bfloat16) for k in range(tiles)]
        for j in range(tiles)
    ]
    owned = [
        [weight(owner_ref[t] == q, jnp.float32) for q in range(n_layer)] for t in range(n_layer)
    ]
    t2_copies[0].wait()
    expand(0)
    pl.semaphore_wait(barrier, 2 + n_layer - 1)
    hop(0, 0).start()
    t2_copies[1].wait()
    for c in range(1, chunks):
        expand(c)
        if c < AHEAD:
            hop(0, c).start()

    hops = stops - 1
    for step in range(chunks + hops - 1):
        for s in range(1, hops):
            c = step - (s - 1)
            if 0 <= c < chunks:
                hop(s - 1, c).wait_recv()
                hop(s, c).start()
        if step + AHEAD < chunks:
            hop(0, step + AHEAD).start()
        if step == 0:
            slab_copies[0].wait()
        if step < chunks:
            multiply(0, step, True)
        for s in range(1, hops):
            c = step - (s - 1)
            if c == 0:
                slab_copies[s].wait()
            if 0 <= c < chunks:
                multiply(s, c, False)
        c = step - (hops - 1)
        if c == 0:
            slab_copies[hops].wait()
        if 0 <= c < chunks:
            hop(hops - 1, c).wait_recv()
            multiply(hops, c, False)
            to_slots(c)
            for d in range(n_layer - 1):
                give(d, c).start()
        if 0 <= c - 2 < chunks:
            finish(c - 2)
    for c in range(max(chunks - 2, 0), chunks):
        finish(c)
    for c in range(chunks):
        for s in range(hops):
            hop(s, c).wait_send()
        for d in range(n_layer - 1):
            give(d, c).wait_send()


def body(n_blk, n_layer, t2, tile_ids, counts, integrals, owner):
    row_count, width = t2.shape[0], t2.shape[3]
    stops, tiles, tile, cols = integrals.shape[2:]
    tile_rows = row_count // n_layer
    first = SIXTEENTHS[0] * tile_rows // 16
    most = max(SIXTEENTHS) * tile_rows // 16
    chunks = len(SIXTEENTHS)
    hops = stops - 1
    moved = 2 * stops * width * cols + 2 * row_count * width
    result = pl.pallas_call(
        functools.partial(kernel, n_blk, n_layer),
        out_shape=pltpu.VMEM((tile_rows, cols), jnp.bfloat16),
        in_specs=[pl.BlockSpec(memory_space=pltpu.SMEM)] * 3 + [pl.BlockSpec(memory_space=pl.ANY)] * 2,
        out_specs=pl.BlockSpec(memory_space=pltpu.VMEM),
        scratch_shapes=[
            pltpu.VMEM((n_layer, first, width), jnp.bfloat16),
            pltpu.VMEM((n_layer, tile_rows - first, width), jnp.bfloat16),
            pltpu.VMEM((stops, row_count, width), jnp.bfloat16),
            pltpu.VMEM((stops, width, cols), jnp.bfloat16),
            pltpu.VMEM((ACC_SLOTS, n_layer * most, cols), jnp.float32),
            pltpu.VMEM((n_layer, tile_rows, cols), jnp.float32),
            pltpu.VMEM((n_layer - 1, tile_rows, cols), jnp.float32),
            pltpu.SemaphoreType.DMA((2,)),
            pltpu.SemaphoreType.DMA((stops,)),
            pltpu.SemaphoreType.DMA((hops, chunks)),
            pltpu.SemaphoreType.DMA((hops, chunks)),
            pltpu.SemaphoreType.DMA((n_layer - 1, chunks)),
            pltpu.SemaphoreType.DMA((n_layer - 1, chunks)),
        ],
        compiler_params=pltpu.CompilerParams(
            collective_id=0, has_side_effects=True, vmem_limit_bytes=60 * 2**20
        ),
        cost_estimate=pl.CostEstimate(
            flops=2 * stops * row_count * width * cols, bytes_accessed=moved, transcendentals=0
        ),
    )(
        tile_ids.reshape(tiles),
        counts.reshape(1),
        owner.reshape(n_layer),
        t2.reshape(n_layer, tile_rows, width),
        integrals.reshape(stops, tiles * tile, cols),
    )
    return result.reshape(1, tile_rows, 1, cols)


def solution(mesh):
    return jax.shard_map(
        functools.partial(body, mesh.shape["blk"], mesh.shape["layer"]),
        mesh=mesh,
        in_specs=(
            P(None, "blk", "layer", None),
            P("blk", "layer", None),
            P("blk", "layer"),
            P("blk", "layer", None, None, None, None),
            P("blk", None),
        ),
        out_specs=P("layer", None, "blk", None),
        check_vma=False,
    )
```

```python
import functools

import jax
import jax.numpy as jnp
from jax import lax
from jax.experimental import pallas as pl
from jax.experimental.pallas import tpu as pltpu
from jax.sharding import PartitionSpec as P

MESH = pl.DeviceIdType.MESH
LANES = 256
ACC_SLOTS = 4
AHEAD = 2
SIXTEENTHS = (1, 2, 2, 2, 2, 2, 2, 1, 1, 1)


def kernel(
    n_blk,
    n_layer,
    ids_ref,
    counts_ref,
    owner_ref,
    t2_ref,
    ints_ref,
    out_ref,
    head,
    rest,
    panels,
    slab,
    acc,
    stage,
    landed,
    t2_sem,
    slab_sem,
    ring_send,
    ring_recv,
    sum_send,
    sum_recv,
):
    stops = ints_ref.shape[0]
    tile_rows, width = t2_ref.shape[1], t2_ref.shape[2]
    cols = ints_ref.shape[2]
    tiles = ids_ref.shape[0]
    tile = width // tiles
    sizes = [part * tile_rows // 16 for part in SIXTEENTHS]
    starts = [sum(sizes[:c]) for c in range(len(sizes))]
    chunks = len(sizes)
    lanes = min(LANES, cols)
    blk, layer = lax.axis_index("blk"), lax.axis_index("layer")
    right, left = lax.rem(blk + 1, n_blk), lax.rem(blk + n_blk - 1, n_blk)
    others = [lax.rem(layer + d, n_layer) for d in range(1, n_layer)]

    barrier = pltpu.get_barrier_semaphore()
    for neighbour in (left, right):
        pl.semaphore_signal(barrier, inc=1, device_id={"blk": neighbour}, device_id_type=MESH)
    for other in others:
        pl.semaphore_signal(barrier, inc=1, device_id={"layer": other}, device_id_type=MESH)

    t2_copies = [
        pltpu.make_async_copy(t2_ref.at[:, pl.ds(0, sizes[0])], head, t2_sem.at[0]),
        pltpu.make_async_copy(
            t2_ref.at[:, pl.ds(sizes[0], tile_rows - sizes[0])], rest, t2_sem.at[1]
        ),
    ]
    slab_copies = [
        pltpu.make_async_copy(ints_ref.at[s], slab.at[s], slab_sem.at[s]) for s in range(stops)
    ]
    for copy in t2_copies + slab_copies:
        copy.start()

    count = counts_ref[0]

    def weight(condition, dtype):
        return jnp.full((1, tile), condition.astype(jnp.float32), jnp.float32).astype(dtype)

    def span(c):
        return pl.ds(n_layer * starts[c], n_layer * sizes[c])

    def expand(c):
        source, at = (head, 0) if c == 0 else (rest, starts[c] - sizes[0])
        pieces = [
            source[:, pl.ds(at, sizes[c]), j * tile : (j + 1) * tile].reshape(n_layer * sizes[c], tile)
            for j in range(tiles)
        ]
        for k in range(tiles):
            placed = pieces[0] * held[0][k]
            for j in range(1, tiles):
                placed = placed + pieces[j] * held[j][k]
            panels[0, span(c), k * tile : (k + 1) * tile] = placed

    def to_slots(c):
        for q in range(n_layer):
            for n in range(cols // tile):
                at = slice(n * tile, (n + 1) * tile)
                moved = acc[c % ACC_SLOTS, pl.ds(0, sizes[c]), at] * owned[0][q]
                for t in range(1, n_layer):
                    moved = moved + acc[c % ACC_SLOTS, pl.ds(t * sizes[c], sizes[c]), at] * owned[t][q]
                stage[q, pl.ds(starts[c], sizes[c]), at] = moved

    def hop(s, c):
        return pltpu.make_async_remote_copy(
            src_ref=panels.at[s, span(c)],
            dst_ref=panels.at[s + 1, span(c)],
            send_sem=ring_send.at[s, c],
            recv_sem=ring_recv.at[s, c],
            device_id={"blk": right},
            device_id_type=MESH,
        )

    def give(d, c):
        return pltpu.make_async_remote_copy(
            src_ref=stage.at[others[d], pl.ds(starts[c], sizes[c])],
            dst_ref=landed.at[d, pl.ds(starts[c], sizes[c])],
            send_sem=sum_send.at[d, c],
            recv_sem=sum_recv.at[d, c],
            device_id={"layer": others[d]},
            device_id_type=MESH,
        )

    def multiply(s, c, first):
        @pl.loop(0, cols // lanes)
        def _(n):
            at = pl.ds(pl.multiple_of(n * lanes, lanes), lanes)
            product = jnp.dot(
                panels[s, span(c)], slab[s, :, at], preferred_element_type=jnp.float32
            )
            if first:
                acc[c % ACC_SLOTS, pl.ds(0, n_layer * sizes[c]), at] = product
            else:
                acc[c % ACC_SLOTS, pl.ds(0, n_layer * sizes[c]), at] += product

    def finish(c):
        for d in range(n_layer - 1):
            give(d, c).wait_recv()
        at = pl.ds(starts[c], sizes[c])
        total = stage[layer, at]
        for d in range(n_layer - 1):
            total = total + landed[d, at]
        out_ref[at, :] = total.astype(out_ref.dtype)

    held = [
        [weight((ids_ref[j] == k) & (j < count), jnp.bfloat16) for k in range(tiles)]
        for j in range(tiles)
    ]
    owned = [
        [weight(owner_ref[t] == q, jnp.float32) for q in range(n_layer)] for t in range(n_layer)
    ]
    t2_copies[0].wait()
    expand(0)
    pl.semaphore_wait(barrier, 2 + n_layer - 1)
    hop(0, 0).start()
    t2_copies[1].wait()
    for c in range(1, chunks):
        expand(c)
        if c < AHEAD:
            hop(0, c).start()

    hops = stops - 1
    for step in range(chunks + hops - 1):
        for s in range(hops - 1, 0, -1):
            c = step - (s - 1)
            if 0 <= c < chunks:
                hop(s - 1, c).wait_recv()
                hop(s, c).start()
        if step + AHEAD < chunks:
            hop(0, step + AHEAD).start()
        if step == 0:
            slab_copies[0].wait()
        if step < chunks:
            multiply(0, step, True)
        for s in range(1, hops):
            c = step - (s - 1)
            if c == 0:
                slab_copies[s].wait()
            if 0 <= c < chunks:
                multiply(s, c, False)
        c = step - (hops - 1)
        if c == 0:
            slab_copies[hops].wait()
        if 0 <= c < chunks:
            hop(hops - 1, c).wait_recv()
            multiply(hops, c, False)
            to_slots(c)
            for d in range(n_layer - 1):
                give(d, c).start()
        if 0 <= c - 2 < chunks:
            finish(c - 2)
    for c in range(max(chunks - 2, 0), chunks):
        finish(c)
    for c in range(chunks):
        for s in range(hops):
            hop(s, c).wait_send()
        for d in range(n_layer - 1):
            give(d, c).wait_send()


def body(n_blk, n_layer, t2, tile_ids, counts, integrals, owner):
    row_count, width = t2.shape[0], t2.shape[3]
    stops, tiles, tile, cols = integrals.shape[2:]
    tile_rows = row_count // n_layer
    first = SIXTEENTHS[0] * tile_rows // 16
    most = max(SIXTEENTHS) * tile_rows // 16
    chunks = len(SIXTEENTHS)
    hops = stops - 1
    moved = 2 * stops * width * cols + 2 * row_count * width
    result = pl.pallas_call(
        functools.partial(kernel, n_blk, n_layer),
        out_shape=pltpu.VMEM((tile_rows, cols), jnp.bfloat16),
        in_specs=[pl.BlockSpec(memory_space=pltpu.SMEM)] * 3 + [pl.BlockSpec(memory_space=pl.ANY)] * 2,
        out_specs=pl.BlockSpec(memory_space=pltpu.VMEM),
        scratch_shapes=[
            pltpu.VMEM((n_layer, first, width), jnp.bfloat16),
            pltpu.VMEM((n_layer, tile_rows - first, width), jnp.bfloat16),
            pltpu.VMEM((stops, row_count, width), jnp.bfloat16),
            pltpu.VMEM((stops, width, cols), jnp.bfloat16),
            pltpu.VMEM((ACC_SLOTS, n_layer * most, cols), jnp.float32),
            pltpu.VMEM((n_layer, tile_rows, cols), jnp.float32),
            pltpu.VMEM((n_layer - 1, tile_rows, cols), jnp.float32),
            pltpu.SemaphoreType.DMA((2,)),
            pltpu.SemaphoreType.DMA((stops,)),
            pltpu.SemaphoreType.DMA((hops, chunks)),
            pltpu.SemaphoreType.DMA((hops, chunks)),
            pltpu.SemaphoreType.DMA((n_layer - 1, chunks)),
            pltpu.SemaphoreType.DMA((n_layer - 1, chunks)),
        ],
        compiler_params=pltpu.CompilerParams(
            collective_id=0, has_side_effects=True, vmem_limit_bytes=60 * 2**20
        ),
        cost_estimate=pl.CostEstimate(
            flops=2 * stops * row_count * width * cols, bytes_accessed=moved, transcendentals=0
        ),
    )(
        tile_ids.reshape(tiles),
        counts.reshape(1),
        owner.reshape(n_layer),
        t2.reshape(n_layer, tile_rows, width),
        integrals.reshape(stops, tiles * tile, cols),
    )
    return result.reshape(1, tile_rows, 1, cols)


def solution(mesh):
    return jax.shard_map(
        functools.partial(body, mesh.shape["blk"], mesh.shape["layer"]),
        mesh=mesh,
        in_specs=(
            P(None, "blk", "layer", None),
            P("blk", "layer", None),
            P("blk", "layer"),
            P("blk", "layer", None, None, None, None),
            P("blk", None),
        ),
        out_specs=P("layer", None, "blk", None),
        check_vma=False,
    )
```
